32 devices in a mesh: groups: 2 (over y), edge: 16 (over z, x, core).
Axes of the slice: x: 2, y: 2, z: 4, core: 2. Of those that a mesh axis runs over, the one named last changes fastest.
Arguments:
- nodes: float32 [512, 512], P(('groups', 'edge')), parts along dimension 0, may hold values from -6 to 6
- edge_feat: float32 [24576, 512], P(('groups', 'edge')), parts along dimension 0, may hold values from -6 to 6
- source: int32 [24576], P(('groups', 'edge')), parts along dimension 0, may hold values from 0 to 255, as said below
- target: int32 [24576], P(('groups', 'edge')), parts along dimension 0, may hold values from 0 to 255, as said below
- w_in: float32 [1536, 512], replicated, may hold values from -0.15625 to 0.15625
- w_out: float32 [512, 512], replicated, may hold values from -0.25 to 0.25
- cotangent: float32 [512, 512], P(('groups', 'edge')), parts along dimension 0, may hold values from -6 to 6
Outputs:
- grad_nodes: float32 [512, 512], P(('groups', 'edge')), parts along dimension 0
- grad_in: float32 [3072, 512], P('groups'), parts along dimension 0
- grad_out: float32 [1024, 512], P('groups'), parts along dimension 0
The draws below stay inside these ranges and needn't reach their ends.
There are 2 independent parts, one for each index of `groups`. The reference program is written for one: setup_inputs(seed, part) draws one part's arguments, and reference() takes and returns one part's arrays. A program takes and returns all parts, laid end to end along the dimension named above; an argument that names none is the same for every part. Nothing has to cross between parts.
Inputs may be any that keep to these rules, and one draw needn't show every extreme that they name: `source`: the edges held by one index d of edge (positions d * 768 to (d + 1) * 768 - 1) have at most 96 sources among the nodes held by any one index (nodes j * 16 to (j + 1) * 16 - 1); one index j, the same for all d, holds exactly 96 of the sources of every d. Every edge's target is a node held by the same index of edge as the edge: for positions d * 768 to (d + 1) * 768 - 1 it lies in d * 16 to (d + 1) * 16 - 1.
All inputs are finite; a program needn't handle non-finite values.
Results may differ from the reference program's by a relative error of at most 0.0001.
Values sent between devices are 32-bit elements; how exact they have to be, the bound alone decides.
A program may use at most 64 MiB of HBM per device.

```python
import math
import jax
import jax.numpy as jnp
from jax import lax

H = 512
F = 512
NODE_DEV = 16
EDGE_DEV = 768
NODES = 256
EDGES = 12288
CAP = 96
N_EDGE = 16


def draw_source(key, part):
    key = jax.random.fold_in(key, 11)
    slots = N_EDGE * CAP
    full_owner = jax.random.randint(jax.random.fold_in(key, 1), (), 0, N_EDGE)
    slot_owner = jnp.arange(slots, dtype=jnp.int32) // CAP

    def one_device(dev_key):
        ranks = jax.random.permutation(jax.random.fold_in(dev_key, 1), slots).astype(jnp.int32)
        score = ranks - jnp.where(slot_owner == full_owner, slots, 0).astype(jnp.int32)
        chosen = jnp.argsort(score, stable=True)[:EDGE_DEV].astype(jnp.int32)
        owners = chosen // CAP
        shuffle = jax.random.permutation(jax.random.fold_in(dev_key, 2), EDGE_DEV)
        owners = owners[shuffle]
        offsets = jax.random.randint(jax.random.fold_in(dev_key, 3), (EDGE_DEV,), 0, NODE_DEV)
        return (owners * NODE_DEV + offsets).astype(jnp.int32)
    keys = jax.random.split(jax.random.fold_in(key, 2), N_EDGE)
    return jax.vmap(one_device)(keys).reshape(-1)


def draw_target(key, part):
    key = jax.random.fold_in(key, 23)
    offsets = jax.random.randint(key, (N_EDGE, EDGE_DEV), 0, NODE_DEV)
    owners = jnp.arange(N_EDGE, dtype=jnp.int32)[:, None] * NODE_DEV
    return (owners + offsets).astype(jnp.int32).reshape(-1)


def block_scale(key, shape, cuts, smallest, high):
    loudness, own = 1.0, jax.random.fold_in(key, 6)
    for position, parts in cuts:
        heights = jnp.exp(jax.random.uniform(jax.random.fold_in(own, position), (parts,), jnp.float32, smallest / len(cuts), high / len(cuts)))
        loudness = loudness * jnp.repeat(heights, shape[position] // parts).reshape([-1 if axis == position else 1 for axis in range(len(shape))])
    return loudness


def gaussian(key, shape, spread, limit, cuts=(), kind=jnp.bfloat16):
    level = block_scale(key, shape, cuts, -0.22, 0.18) if cuts else 1.0
    drawn = jax.random.normal(key, shape, jnp.float32) * spread * level
    return jnp.minimum(jnp.maximum(drawn, -limit), limit).astype(kind)


def setup_inputs(seed: int = 0, part: int = 0) -> dict:
    key_list = jax.random.split(jax.random.key(seed), 8)
    part_splits = jax.random.split(jax.random.fold_in(key_list[7], part), 8)
    nodes = gaussian(part_splits[0], (NODES, H), 1.0, 6.0, ((0, 16),), jnp.float32)
    edge_feat = gaussian(part_splits[1], (EDGES, H), 1.0, 6.0, ((0, 16),), jnp.float32)
    source = draw_source(jax.random.fold_in(jax.random.fold_in(key_list[7], part), 71), part)
    target = draw_target(jax.random.fold_in(jax.random.fold_in(key_list[7], part), 71), part)
    w_in = gaussian(key_list[4], (3 * H, F), (3 * H) ** -0.5, 0.15625, (), jnp.float32)
    w_out = gaussian(key_list[5], (F, H), F ** -0.5, 0.25, (), jnp.float32)
    cotangent = gaussian(part_splits[6], (NODES, H), 1.0, 6.0, ((0, 16),), jnp.float32)
    return {"nodes": nodes, "edge_feat": edge_feat, "source": source, "target": target, "w_in": w_in, "w_out": w_out, "cotangent": cotangent}


def reference(nodes, edge_feat, source, target, w_in, w_out, cotangent):
    width = nodes.shape[1]
    highest = lax.Precision.HIGHEST
    blocks = source.shape[0] // EDGE_DEV
    src_blocks = source.reshape(blocks, EDGE_DEV).astype(jnp.int32)
    dst_blocks = target.reshape(blocks, EDGE_DEV).astype(jnp.int32)
    feat_blocks = edge_feat.reshape(blocks, EDGE_DEV, width)

    def visit(carry, pieces):
        grads, grad_first, grad_second = carry
        src, dst, feats = pieces
        inputs = jnp.concatenate([nodes[src], nodes[dst], feats], axis=1)
        preact = jnp.dot(inputs, w_in, precision=highest, preferred_element_type=jnp.float32)
        sigma = jax.nn.sigmoid(preact)
        hidden = preact * sigma
        upstream = cotangent[dst]
        back = jnp.dot(upstream, w_out.T, precision=highest, preferred_element_type=jnp.float32)
        dpre = back * sigma * (1.0 + preact * (1.0 - sigma))
        dinputs = jnp.dot(dpre, w_in.T, precision=highest, preferred_element_type=jnp.float32)
        grad_first = grad_first + jnp.dot(inputs.T, dpre, precision=highest, preferred_element_type=jnp.float32)
        grad_second = grad_second + jnp.dot(hidden.T, upstream, precision=highest, preferred_element_type=jnp.float32)
        grads = grads.at[src].add(dinputs[:, :width]).at[dst].add(dinputs[:, width:2 * width])
        return ((grads, grad_first, grad_second), None)
    start = (jnp.zeros(nodes.shape, jnp.float32), jnp.zeros(w_in.shape, jnp.float32), jnp.zeros(w_out.shape, jnp.float32))
    (grads, grad_first, grad_second), _ = lax.scan(visit, start, (src_blocks, dst_blocks, feat_blocks))
    factor = 1.0 / math.sqrt(source.shape[0])
    return (grads, grad_first * factor, grad_second * factor)
```

```python
import functools
import math

import jax
import jax.numpy as jnp
from jax import lax
from jax.experimental import pallas as pl
from jax.experimental.pallas import tpu as pltpu
from jax.sharding import PartitionSpec as P


def plain(nodes, edge_feat, source, target, w_in, w_out, cotangent):
    highest = lax.Precision.HIGHEST
    node_rows, width = nodes.shape
    edge_rows = source.shape[0]
    devices = lax.axis_size("edge")
    first_node = lax.axis_index("edge") * node_rows
    local_hot = (
        target[:, None] - first_node == jnp.arange(node_rows, dtype=jnp.int32)[None, :]
    ).astype(jnp.float32)
    near = jnp.dot(local_hot, nodes, precision=highest, preferred_element_type=jnp.float32)
    upstream = jnp.dot(local_hot, cotangent, precision=highest, preferred_element_type=jnp.float32)
    w_source = w_in[:width]
    table = jnp.dot(nodes, w_source, precision=highest, preferred_element_type=jnp.float32)
    piece = lax.all_gather(table, "edge", axis=0, tiled=True)
    count = piece.shape[0]
    hot = (source[:, None] == jnp.arange(count, dtype=jnp.int32)[None, :]).astype(jnp.float32)
    far = jnp.dot(hot, piece, precision=highest, preferred_element_type=jnp.float32)
    rest = jnp.concatenate([near, edge_feat], axis=1)
    preact = far + jnp.dot(
        rest, w_in[width:], precision=highest, preferred_element_type=jnp.float32
    )
    sigma = jax.nn.sigmoid(preact)
    hidden = preact * sigma
    back = jnp.dot(upstream, w_out.T, precision=highest, preferred_element_type=jnp.float32)
    dpre = back * sigma * (1.0 + preact * (1.0 - sigma))
    grad_second = jnp.dot(hidden.T, upstream, precision=highest, preferred_element_type=jnp.float32)
    grad_rest = jnp.dot(rest.T, dpre, precision=highest, preferred_element_type=jnp.float32)
    drest = jnp.dot(dpre, w_in[width:].T, precision=highest, preferred_element_type=jnp.float32)
    hot = (
        source[:, None] == jnp.arange(lax.axis_size("edge") * node_rows, dtype=jnp.int32)[None, :]
    ).astype(jnp.float32)
    source_sum = lax.psum_scatter(
        jnp.einsum("ec,ew->cw", hot, dpre, precision=highest, preferred_element_type=jnp.float32),
        "edge",
        scatter_dimension=0,
        tiled=True,
    )
    grad_source = jnp.dot(
        source_sum, w_source.T, precision=highest, preferred_element_type=jnp.float32
    )
    grad_top = jnp.dot(nodes.T, source_sum, precision=highest, preferred_element_type=jnp.float32)
    grad_first = jnp.concatenate([grad_top, grad_rest], axis=0)
    near_grad = drest[:, :width]
    grads = grad_source + jnp.einsum(
        "en,ew->nw", local_hot, near_grad, precision=highest, preferred_element_type=jnp.float32
    )
    grad_first, grad_second = lax.psum((grad_first, grad_second), "edge")
    factor = 1.0 / math.sqrt(edge_rows * devices)
    return (grads, grad_first * factor, grad_second * factor)


MESH = pl.DeviceIdType.MESH
NODE, COT, TGT, HID, SRC, FA, FB = range(7)


def split(value):
    high = value.astype(jnp.bfloat16)
    low = (value - high.astype(jnp.float32)).astype(jnp.bfloat16)
    return high, low


def mm(a, b, dims=((1,), (0,))):
    return lax.dot_general(a, b, (dims, ((), ())), preferred_element_type=jnp.float32)


def mm3(a, b, dims=((1,), (0,))):
    (ah, al), (bh, bl) = a, b
    return mm(ah, bh, dims) + (mm(ah, bl, dims) + mm(al, bh, dims))


def kernel(n, nodes, cot, src, tgt, feat_hbm, win_hbm, wout_hbm, grads, gin, gout,
           ag, part, rc, rx, rz, feat, win, wout, eth, etl, hot_t, hot,
           tabh, tabl, bkh, bkl, pre, dh, dl, ngth, ngtl, load_sem, send_sem, recv_sem):
    f32, bf16 = jnp.float32, jnp.bfloat16
    rows, width = nodes.shape
    edges = src.shape[1]
    zs = n // 4
    total = n * rows
    factor = 1.0 / math.sqrt(edges * n)
    me = lax.axis_index("edge")
    c, x, z = lax.rem(me, 2), lax.rem(me // 2, 2), me // 4

    def index(z, x, c):
        return (z * 2 + x) * 2 + c

    sibling, across = index(z, x, 1 - c), index(z, 1 - x, c)
    line = [index(lax.rem(z + k, zs), x, c) for k in range(1, zs)]
    half, quarter = total // 2, total // 4

    def at(size, start):
        return pl.ds(pl.multiple_of(start, rows), size)

    own = at(rows, c * half + x * quarter + z * rows)
    sent = {}

    def send(key, slot, source, dest, device):
        copy = pltpu.make_async_remote_copy(
            src_ref=source, dst_ref=dest, send_sem=send_sem.at[slot], recv_sem=recv_sem.at[slot],
            device_id={"edge": device}, device_id_type=MESH)
        copy.start()
        sent.setdefault(key, []).append(copy)

    def fin(*key):
        for copy in sent[key]:
            copy.wait_recv()

    per = zs + 1

    def ag_z(i):
        for k, device in enumerate(line):
            send(("az", i), i * per + k, ag.at[i, own], ag.at[i, own], device)

    def ag_x(i):
        fin("az", i)
        block = at(quarter, c * half + x * quarter)
        send(("ax", i), i * per + zs - 1, ag.at[i, block], ag.at[i, block], across)

    def ag_c(i):
        fin("ax", i)
        block = at(half, c * half)
        send(("ac", i), i * per + zs, ag.at[i, block], ag.at[i, block], sibling)

    def rs_c(j):
        send(("rc", j), (7 + j) * per, part.at[j, at(half, (1 - c) * half)], rc.at[j], sibling)

    def rs_x(j):
        fin("rc", j)
        away = at(quarter, c * half + (1 - x) * quarter)
        part[j, away] += rc[j, at(quarter, (1 - x) * quarter)]
        send(("rx", j), (7 + j) * per + 1, part.at[j, away], rx.at[j], across)
        part[j, at(quarter, c * half + x * quarter)] += rc[j, at(quarter, x * quarter)]

    def rs_z(j):
        fin("rx", j)
        base = c * half + x * quarter
        part[j, at(quarter, base)] += rx[j]
        for k, device in enumerate(line):
            other = lax.rem(z + k + 1, zs)
            send(("rz", j), (7 + j) * per + 2 + k, part.at[j, at(rows, base + other * rows)],
                 rz.at[j, k], device)

    def rs_done(j, i):
        fin("rz", j)
        piece = part[j, own]
        for k in range(zs - 1):
            piece = piece + rz[j, k]
        ag[i, own] = piece
        ag_z(i)

    load_feat = pltpu.make_async_copy(feat_hbm, feat, load_sem.at[0])
    load_win = pltpu.make_async_copy(win_hbm, win, load_sem.at[1])
    load_wout = pltpu.make_async_copy(wout_hbm, wout, load_sem.at[2])
    load_feat.start()
    load_win.start()
    load_wout.start()
    ag[NODE, own] = nodes[...]
    ag[COT, own] = cot[...]
    barrier = pltpu.get_barrier_semaphore()
    peers = [sibling, across] + line
    for device in peers:
        pl.semaphore_signal(barrier, inc=1, device_id={"edge": device}, device_id_type=MESH)
    pl.semaphore_wait(barrier, len(peers))
    ag_z(NODE)

    ids = src[...]
    owner = ids // rows
    place = (lax.rem(owner, 2) * half + lax.rem(owner // 2, 2) * quarter
             + (owner // 4) * rows + lax.rem(ids, rows))
    seen = lax.broadcasted_iota(jnp.int32, (total, edges), 0) == place
    near = lax.broadcasted_iota(jnp.int32, (128, edges), 0) == tgt[...] - me * rows
    seen, near = jnp.where(seen, 1.0, 0.0), jnp.where(near, 1.0, 0.0)
    hot_t[0:total] = seen.astype(bf16)
    hot_t[total:total + 128] = near.astype(bf16)
    hot[:, 0:total] = seen.T.astype(bf16)
    hot[:, total:total + 128] = near.T.astype(bf16)

    load_feat.wait()
    load_win.wait()
    tile = 256
    tiles = edges // tile

    def first(t):
        high, low = split(feat[t * tile:(t + 1) * tile])
        wf = split(win[2 * width:3 * width])
        pre[t * tile:(t + 1) * tile] = mm3((high, low), wf)

    def turn(t):
        high, low = split(feat[t * tile:(t + 1) * tile].T)
        eth[:, t * tile:(t + 1) * tile] = high
        etl[:, t * tile:(t + 1) * tile] = low

    first(0)
    ag_x(NODE)
    ag_z(COT)
    first(1)
    ag_c(NODE)
    first(2)
    load_wout.wait()
    zeros = jnp.zeros((128 - rows, width), bf16)
    th, tl = split(mm3(split(nodes[...]), split(win[width:2 * width])))
    tabh[total:total + 128] = jnp.concatenate([th, zeros], axis=0)
    tabl[total:total + 128] = jnp.concatenate([tl, zeros], axis=0)
    th, tl = split(mm3(split(cot[...]), split(wout[...]), ((1,), (1,))))
    bkh[...] = jnp.concatenate([th, zeros], axis=0)
    bkl[...] = jnp.concatenate([tl, zeros], axis=0)
    for t in range(tiles):
        turn(t)
    fin("ac", NODE)
    th, tl = split(mm3(split(ag[NODE]), split(win[0:width])))
    tabh[0:total] = th
    tabl[0:total] = tl
    ag_x(COT)

    t_sum = jnp.zeros((rows, width), f32)
    g_sum = jnp.zeros((rows, width), f32)
    for t in range(tiles):
        cut = slice(t * tile, (t + 1) * tile)
        ones = hot[cut]
        v = pre[cut] + (mm(ones, tabh[...]) + mm(ones, tabl[...]))
        back = mm(ones[:, total:], bkh[...]) + mm(ones[:, total:], bkl[...])
        sigma = jax.nn.sigmoid(v)
        hh, hl = split(v * sigma)
        high, low = split(back * sigma * (1.0 + v * (1.0 - sigma)))
        dh[cut] = high
        dl[cut] = low
        ones_t = hot_t[total:total + rows, cut]
        t_sum += mm(ones_t, high) + mm(ones_t, low)
        g_sum += mm(ones_t, hh) + mm(ones_t, hl)
    ag[TGT, own] = t_sum
    ag[HID, own] = g_sum
    ag_z(TGT)
    ag_z(HID)
    part[0] = mm(hot_t[0:total], dh[...]) + mm(hot_t[0:total], dl[...])
    rs_c(0)
    ag_c(COT)

    def outer(j):
        cut = slice((j - 1) * total, j * total)
        part[j] = mm3((eth[cut], etl[cut]), (dh[...], dl[...]))
        rs_c(j)

    outer(1)
    rs_x(0)
    outer(2)
    rs_x(1)
    rs_z(0)
    rs_x(2)
    ag_x(TGT)
    ag_x(HID)
    nh, nl = split(ag[NODE].T)
    ngth[...] = nh
    ngtl[...] = nl
    rs_z(1)
    rs_done(0, SRC)
    rs_z(2)
    ag_c(TGT)
    ag_c(HID)
    grads[...] = (mm3(split(ag[SRC, own]), split(win[0:width]), ((1,), (1,)))
                  + mm3(split(ag[TGT, own]), split(win[width:2 * width]), ((1,), (1,))))
    rs_done(1, FA)
    ag_x(SRC)
    rs_done(2, FB)
    fin("ac", TGT)
    gin[width:2 * width] = mm3((ngth[...], ngtl[...]), split(ag[TGT])) * factor
    ag_x(FA)
    ag_c(SRC)
    ag_x(FB)
    fin("ac", HID)
    fin("ac", COT)
    gout[...] = mm3(split(ag[HID].T), split(ag[COT])) * factor
    ag_c(FA)
    fin("ac", SRC)
    gin[0:width] = mm3((ngth[...], ngtl[...]), split(ag[SRC])) * factor
    ag_c(FB)
    fin("ac", FA)
    gin[2 * width:2 * width + total] = ag[FA] * factor
    fin("ac", FB)
    gin[2 * width + total:3 * width] = ag[FB] * factor
    for copies in sent.values():
        for copy in copies:
            copy.wait_send()


def fused(n, nodes, edge_feat, source, target, w_in, w_out, cotangent):
    f32, bf16 = jnp.float32, jnp.bfloat16
    rows, width = nodes.shape
    edges = source.shape[0]
    zs, total = n // 4, n * rows
    vmem = pl.BlockSpec(memory_space=pltpu.VMEM)
    hbm = pl.BlockSpec(memory_space=pl.ANY)
    scratch = [
        ((7, total, width), f32), ((3, total, width), f32), ((3, total // 2, width), f32),
        ((3, total // 4, width), f32), ((3, zs - 1, rows, width), f32),
        ((edges, width), f32), ((3 * width, width), f32), ((width, width), f32),
        ((width, edges), bf16), ((width, edges), bf16),
        ((total + 128, edges), bf16), ((edges, total + 128), bf16),
        ((total + 128, width), bf16), ((total + 128, width), bf16),
        ((128, width), bf16), ((128, width), bf16),
        ((edges, width), f32), ((edges, width), bf16), ((edges, width), bf16),
        ((width, total), bf16), ((width, total), bf16),
    ]
    copies = 10 * (zs + 1)
    return pl.pallas_call(
        functools.partial(kernel, n),
        out_shape=(
            jax.ShapeDtypeStruct((rows, width), f32),
            jax.ShapeDtypeStruct((3 * width, width), f32),
            jax.ShapeDtypeStruct((width, width), f32),
        ),
        in_specs=[vmem] * 4 + [hbm] * 3,
        out_specs=(vmem, vmem, vmem),
        scratch_shapes=[pltpu.VMEM(shape, kind) for shape, kind in scratch] + [
            pltpu.SemaphoreType.DMA((3,)),
            pltpu.SemaphoreType.DMA((copies,)),
            pltpu.SemaphoreType.DMA((copies,)),
        ],
        compiler_params=pltpu.CompilerParams(
            collective_id=0, has_side_effects=True, vmem_limit_bytes=52 * 2**20),
    )(nodes, cotangent, source.reshape(1, edges), target.reshape(1, edges), edge_feat, w_in, w_out)


def body(nodes, edge_feat, source, target, w_in, w_out, cotangent):
    devices = lax.axis_size("edge")
    rows, width = nodes.shape
    if devices % 4 == 0 and devices >= 8 and 2 * devices * rows == width and source.shape[0] % 256 == 0:
        return fused(devices, nodes, edge_feat, source, target, w_in, w_out, cotangent)
    return plain(nodes, edge_feat, source, target, w_in, w_out, cotangent)


def solution(mesh):
    placed = (
        P(("groups", "edge"), None),
        P(("groups", "edge"), None),
        P(("groups", "edge")),
        P(("groups", "edge")),
        P(),
        P(),
        P(("groups", "edge"), None),
    )
    return jax.shard_map(
        body,
        mesh=mesh,
        in_specs=placed,
        out_specs=(P(("groups", "edge"), None), P("groups", None), P("groups", None)),
        check_vma=False,
    )
```

```python
import functools
import math

import jax
import jax.numpy as jnp
from jax import lax
from jax.experimental import pallas as pl
from jax.experimental.pallas import tpu as pltpu
from jax.sharding import PartitionSpec as P


def plain(nodes, edge_feat, source, target, w_in, w_out, cotangent):
    highest = lax.Precision.HIGHEST
    node_rows, width = nodes.shape
    edge_rows = source.shape[0]
    devices = lax.axis_size("edge")
    first_node = lax.axis_index("edge") * node_rows
    local_hot = (
        target[:, None] - first_node == jnp.arange(node_rows, dtype=jnp.int32)[None, :]
    ).astype(jnp.float32)
    near = jnp.dot(local_hot, nodes, precision=highest, preferred_element_type=jnp.float32)
    upstream = jnp.dot(local_hot, cotangent, precision=highest, preferred_element_type=jnp.float32)
    w_source = w_in[:width]
    table = jnp.dot(nodes, w_source, precision=highest, preferred_element_type=jnp.float32)
    piece = lax.all_gather(table, "edge", axis=0, tiled=True)
    count = piece.shape[0]
    hot = (source[:, None] == jnp.arange(count, dtype=jnp.int32)[None, :]).astype(jnp.float32)
    far = jnp.dot(hot, piece, precision=highest, preferred_element_type=jnp.float32)
    rest = jnp.concatenate([near, edge_feat], axis=1)
    preact = far + jnp.dot(
        rest, w_in[width:], precision=highest, preferred_element_type=jnp.float32
    )
    sigma = jax.nn.sigmoid(preact)
    hidden = preact * sigma
    back = jnp.dot(upstream, w_out.T, precision=highest, preferred_element_type=jnp.float32)
    dpre = back * sigma * (1.0 + preact * (1.0 - sigma))
    grad_second = jnp.dot(hidden.T, upstream, precision=highest, preferred_element_type=jnp.float32)
    grad_rest = jnp.dot(rest.T, dpre, precision=highest, preferred_element_type=jnp.float32)
    drest = jnp.dot(dpre, w_in[width:].T, precision=highest, preferred_element_type=jnp.float32)
    hot = (
        source[:, None] == jnp.arange(lax.axis_size("edge") * node_rows, dtype=jnp.int32)[None, :]
    ).astype(jnp.float32)
    source_sum = lax.psum_scatter(
        jnp.einsum("ec,ew->cw", hot, dpre, precision=highest, preferred_element_type=jnp.float32),
        "edge",
        scatter_dimension=0,
        tiled=True,
    )
    grad_source = jnp.dot(
        source_sum, w_source.T, precision=highest, preferred_element_type=jnp.float32
    )
    grad_top = jnp.dot(nodes.T, source_sum, precision=highest, preferred_element_type=jnp.float32)
    grad_first = jnp.concatenate([grad_top, grad_rest], axis=0)
    near_grad = drest[:, :width]
    grads = grad_source + jnp.einsum(
        "en,ew->nw", local_hot, near_grad, precision=highest, preferred_element_type=jnp.float32
    )
    grad_first, grad_second = lax.psum((grad_first, grad_second), "edge")
    factor = 1.0 / math.sqrt(edge_rows * devices)
    return (grads, grad_first * factor, grad_second * factor)


MESH = pl.DeviceIdType.MESH
NODE, COT, TGT, HID, SRC, FA, FB = range(7)


def split(value):
    high = value.astype(jnp.bfloat16)
    low = (value - high.astype(jnp.float32)).astype(jnp.bfloat16)
    return high, low


def mm(a, b, dims=((1,), (0,))):
    return lax.dot_general(a, b, (dims, ((), ())), preferred_element_type=jnp.float32)


def mm3(a, b, dims=((1,), (0,))):
    (ah, al), (bh, bl) = a, b
    return mm(ah, bh, dims) + (mm(ah, bl, dims) + mm(al, bh, dims))


def kernel(n, nodes, cot, src_hbm, tgt_hbm, feat, win, wout, grads, gin, gout,
           ag, part, rc, rx, rz, eth, etl, hot_t, hot,
           tabh, tabl, bkh, bkl, pre, dh, dl, ngth, ngtl, src, tgt, load_sem, send_sem, recv_sem):
    f32, bf16 = jnp.float32, jnp.bfloat16
    rows, width = nodes.shape
    edges = src.shape[1]
    zs = n // 4
    total = n * rows
    factor = 1.0 / math.sqrt(edges * n)
    me = lax.axis_index("edge")
    c, x, z = lax.rem(me, 2), lax.rem(me // 2, 2), me // 4

    def index(z, x, c):
        return (z * 2 + x) * 2 + c

    sibling, across = index(z, x, 1 - c), index(z, 1 - x, c)
    line = [index(lax.rem(z + k, zs), x, c) for k in range(1, zs)]
    half, quarter = total // 2, total // 4

    def at(size, start):
        return pl.ds(pl.multiple_of(start, rows), size)

    own = at(rows, c * half + x * quarter + z * rows)
    sent = {}

    def send(key, slot, source, dest, device):
        copy = pltpu.make_async_remote_copy(
            src_ref=source, dst_ref=dest, send_sem=send_sem.at[slot], recv_sem=recv_sem.at[slot],
            device_id={"edge": device}, device_id_type=MESH)
        copy.start()
        sent.setdefault(key, []).append(copy)

    def fin(*key):
        for copy in sent[key]:
            copy.wait_recv()

    per = zs + 1

    def cols(h):
        return pl.ds(0, width) if h is None else pl.ds(h * (width // 2), width // 2)

    def slot(i, h):
        return i * per if not h else (10 + i) * per

    def ag_z(i, h=None):
        for k, device in enumerate(line):
            send(("az", i, h), slot(i, h) + k, ag.at[i, own, cols(h)], ag.at[i, own, cols(h)],
                 device)

    def ag_x(i, h=None):
        fin("az", i, h)
        block = at(quarter, c * half + x * quarter)
        send(("ax", i, h), slot(i, h) + zs - 1, ag.at[i, block, cols(h)], ag.at[i, block, cols(h)],
             across)

    def ag_c(i, h=None):
        fin("ax", i, h)
        block = at(half, c * half)
        send(("ac", i, h), slot(i, h) + zs, ag.at[i, block, cols(h)], ag.at[i, block, cols(h)],
             sibling)

    def rs_c(j):
        send(("rc", j), (7 + j) * per, part.at[j, at(half, (1 - c) * half)], rc.at[j], sibling)

    def rs_x(j):
        fin("rc", j)
        away = at(quarter, c * half + (1 - x) * quarter)
        part[j, away] += rc[j, at(quarter, (1 - x) * quarter)]
        send(("rx", j), (7 + j) * per + 1, part.at[j, away], rx.at[j], across)
        part[j, at(quarter, c * half + x * quarter)] += rc[j, at(quarter, x * quarter)]

    def rs_z(j):
        fin("rx", j)
        base = c * half + x * quarter
        part[j, at(quarter, base)] += rx[j]
        for k, device in enumerate(line):
            other = lax.rem(z + k + 1, zs)
            send(("rz", j), (7 + j) * per + 2 + k, part.at[j, at(rows, base + other * rows)],
                 rz.at[j, k], device)

    def rs_done(j, i):
        fin("rz", j)
        piece = part[j, own]
        for k in range(zs - 1):
            piece = piece + rz[j, k]
        ag[i, own] = piece
        ag_z(i)

    load_small = [
        pltpu.make_async_copy(src_hbm, src.at[0], load_sem.at[0]),
        pltpu.make_async_copy(tgt_hbm, tgt.at[0], load_sem.at[1]),
    ]
    for copy in load_small:
        copy.start()
    barrier = pltpu.get_barrier_semaphore()
    peers = [sibling, across] + line
    for device in peers:
        pl.semaphore_signal(barrier, inc=1, device_id={"edge": device}, device_id_type=MESH)
    ag[NODE, own] = nodes[...]
    ag[COT, own] = cot[...]
    pl.semaphore_wait(barrier, len(peers))
    for h in range(2):
        ag_z(NODE, h)
    for copy in load_small:
        copy.wait()

    ids = src[...]
    owner = ids // rows
    place = (lax.rem(owner, 2) * half + lax.rem(owner // 2, 2) * quarter
             + (owner // 4) * rows + lax.rem(ids, rows))
    seen = lax.broadcasted_iota(jnp.int32, (total, edges), 0) == place
    near = lax.broadcasted_iota(jnp.int32, (128, edges), 0) == tgt[...] - me * rows
    seen, near = jnp.where(seen, 1.0, 0.0), jnp.where(near, 1.0, 0.0)
    hot_t[0:total] = seen.astype(bf16)
    hot_t[total:total + 128] = near.astype(bf16)
    hot[:, 0:total] = seen.T.astype(bf16)
    hot[:, total:total + 128] = near.T.astype(bf16)

    tile = 256
    tiles = edges // tile

    def turn(t):
        high, low = split(feat[t * tile:(t + 1) * tile].T)
        eth[:, t * tile:(t + 1) * tile] = high
        etl[:, t * tile:(t + 1) * tile] = low

    for h in range(2):
        ag_x(NODE, h)
    ag_z(COT)
    pre[...] = mm3(split(feat[...]), split(win[2 * width:3 * width]))
    for h in range(2):
        ag_c(NODE, h)
    zeros = jnp.zeros((128 - rows, width), bf16)
    th, tl = split(mm3(split(nodes[...]), split(win[width:2 * width])))
    tabh[total:total + 128] = jnp.concatenate([th, zeros], axis=0)
    tabl[total:total + 128] = jnp.concatenate([tl, zeros], axis=0)
    th, tl = split(mm3(split(cot[...]), split(wout[...]), ((1,), (1,))))
    bkh[...] = jnp.concatenate([th, zeros], axis=0)
    bkl[...] = jnp.concatenate([tl, zeros], axis=0)
    for t in range(tiles):
        turn(t)
    for h in range(2):
        fin("ac", NODE, h)
    th, tl = split(mm3(split(ag[NODE]), split(win[0:width])))
    tabh[0:total] = th
    tabl[0:total] = tl
    ag_x(COT)

    t_sum = jnp.zeros((rows, width), f32)
    g_sum = jnp.zeros((rows, width), f32)
    for t in range(tiles):
        cut = slice(t * tile, (t + 1) * tile)
        ones = hot[cut]
        v = pre[cut] + (mm(ones, tabh[...]) + mm(ones, tabl[...]))
        back = mm(ones[:, total:], bkh[...]) + mm(ones[:, total:], bkl[...])
        sigma = jax.nn.sigmoid(v)
        hh, hl = split(v * sigma)
        high, low = split(back * sigma * (1.0 + v * (1.0 - sigma)))
        dh[cut] = high
        dl[cut] = low
        ones_t = hot_t[total:total + rows, cut]
        t_sum += mm(ones_t, high) + mm(ones_t, low)
        g_sum += mm(ones_t, hh) + mm(ones_t, hl)
    ag[TGT, own] = t_sum
    ag[HID, own] = g_sum
    ag_z(TGT)
    ag_z(HID)

    def partial(j, side):
        place = at(half, side * half)
        if j == 0:
            ones_t = hot_t[place]
            part[j, place] = mm(ones_t, dh[...]) + mm(ones_t, dl[...])
        else:
            cut = at(half, (j - 1) * total + side * half)
            part[j, place] = mm3((eth[cut], etl[cut]), (dh[...], dl[...]))

    for j in range(3):
        partial(j, 1 - c)
        rs_c(j)
    partial(0, c)
    rs_x(0)
    partial(1, c)
    rs_x(1)
    partial(2, c)
    ag_c(COT)
    rs_z(0)
    rs_x(2)
    ag_x(TGT)
    ag_x(HID)
    nh, nl = split(ag[NODE].T)
    ngth[...] = nh
    ngtl[...] = nl
    rs_z(1)
    rs_done(0, SRC)
    rs_z(2)
    ag_c(TGT)
    ag_c(HID)
    grads[...] = (mm3(split(ag[SRC, own]), split(win[0:width]), ((1,), (1,)))
                  + mm3(split(ag[TGT, own]), split(win[width:2 * width]), ((1,), (1,))))
    rs_done(1, FA)
    ag_x(SRC)
    rs_done(2, FB)
    fin("ac", TGT, None)
    gin[width:2 * width] = mm3((ngth[...], ngtl[...]), split(ag[TGT])) * factor
    ag_x(FA)
    ag_c(SRC)
    ag_x(FB)
    fin("ac", HID, None)
    fin("ac", COT, None)
    gout[...] = mm3(split(ag[HID].T), split(ag[COT])) * factor
    ag_c(FA)
    fin("ac", SRC, None)
    gin[0:width] = mm3((ngth[...], ngtl[...]), split(ag[SRC])) * factor
    ag_c(FB)
    fin("ac", FA, None)
    gin[2 * width:2 * width + total] = ag[FA] * factor
    fin("ac", FB, None)
    gin[2 * width + total:3 * width] = ag[FB] * factor
    for copies in sent.values():
        for copy in copies:
            copy.wait_send()


def write_out(*refs):
    sem = refs[6]
    copies = [pltpu.make_async_copy(refs[k], refs[3 + k], sem.at[k]) for k in range(3)]
    for copy in copies:
        copy.start()
    for copy in copies:
        copy.wait()


def fused(n, nodes, edge_feat, source, target, w_in, w_out, cotangent):
    f32, bf16 = jnp.float32, jnp.bfloat16
    rows, width = nodes.shape
    edges = source.shape[0]
    zs, total = n // 4, n * rows
    vmem = pl.BlockSpec(memory_space=pltpu.VMEM)
    hbm = pl.BlockSpec(memory_space=pl.ANY)
    scratch = [
        ((7, total, width), f32), ((3, total, width), f32), ((3, total // 2, width), f32),
        ((3, total // 4, width), f32), ((3, zs - 1, rows, width), f32),
        ((width, edges), bf16), ((width, edges), bf16),
        ((total + 128, edges), bf16), ((edges, total + 128), bf16),
        ((total + 128, width), bf16), ((total + 128, width), bf16),
        ((128, width), bf16), ((128, width), bf16),
        ((edges, width), f32), ((edges, width), bf16), ((edges, width), bf16),
        ((width, total), bf16), ((width, total), bf16),
        ((1, edges), jnp.int32), ((1, edges), jnp.int32),
    ]
    copies = 11 * (zs + 1)
    results = pl.pallas_call(
        functools.partial(kernel, n),
        out_shape=(
            jax.ShapeDtypeStruct((rows, width), f32),
            jax.ShapeDtypeStruct((3 * width, width), f32),
            jax.ShapeDtypeStruct((width, width), f32),
        ),
        in_specs=[vmem] * 2 + [hbm] * 2 + [vmem] * 3,
        out_specs=(vmem, vmem, vmem),
        scratch_shapes=[pltpu.VMEM(shape, kind) for shape, kind in scratch] + [
            pltpu.SemaphoreType.DMA((2,)),
            pltpu.SemaphoreType.DMA((copies,)),
            pltpu.SemaphoreType.DMA((copies,)),
        ],
        compiler_params=pltpu.CompilerParams(
            collective_id=0, has_side_effects=True, vmem_limit_bytes=32 * 2**20),
    )(nodes, cotangent, source, target, edge_feat, w_in, w_out)
    return pl.pallas_call(
        write_out,
        out_shape=tuple(jax.ShapeDtypeStruct(r.shape, r.dtype) for r in results),
        in_specs=[hbm] * 3,
        out_specs=(hbm,) * 3,
        scratch_shapes=[pltpu.SemaphoreType.DMA((3,))],
        compiler_params=pltpu.CompilerParams(vmem_limit_bytes=2 * 2**20),
    )(*results)


def body(nodes, edge_feat, source, target, w_in, w_out, cotangent):
    devices = lax.axis_size("edge")
    rows, width = nodes.shape
    if devices % 4 == 0 and devices >= 8 and 2 * devices * rows == width and source.shape[0] % 256 == 0:
        return fused(devices, nodes, edge_feat, source, target, w_in, w_out, cotangent)
    return plain(nodes, edge_feat, source, target, w_in, w_out, cotangent)


def solution(mesh):
    placed = (
        P(("groups", "edge"), None),
        P(("groups", "edge"), None),
        P(("groups", "edge")),
        P(("groups", "edge")),
        P(),
        P(),
        P(("groups", "edge"), None),
    )
    return jax.shard_map(
        body,
        mesh=mesh,
        in_specs=placed,
        out_specs=(P(("groups", "edge"), None), P("groups", None), P("groups", None)),
        check_vma=False,
    )
```

```python
import functools
import math

import jax
import jax.numpy as jnp
from jax import lax
from jax.experimental import pallas as pl
from jax.experimental.pallas import tpu as pltpu
from jax.sharding import PartitionSpec as P


def plain(nodes, edge_feat, source, target, w_in, w_out, cotangent):
    highest = lax.Precision.HIGHEST
    node_rows, width = nodes.shape
    edge_rows = source.shape[0]
    devices = lax.axis_size("edge")
    first_node = lax.axis_index("edge") * node_rows
    local_hot = (
        target[:, None] - first_node == jnp.arange(node_rows, dtype=jnp.int32)[None, :]
    ).astype(jnp.float32)
    near = jnp.dot(local_hot, nodes, precision=highest, preferred_element_type=jnp.float32)
    upstream = jnp.dot(local_hot, cotangent, precision=highest, preferred_element_type=jnp.float32)
    w_source = w_in[:width]
    table = jnp.dot(nodes, w_source, precision=highest, preferred_element_type=jnp.float32)
    piece = lax.all_gather(table, "edge", axis=0, tiled=True)
    count = piece.shape[0]
    hot = (source[:, None] == jnp.arange(count, dtype=jnp.int32)[None, :]).astype(jnp.float32)
    far = jnp.dot(hot, piece, precision=highest, preferred_element_type=jnp.float32)
    rest = jnp.concatenate([near, edge_feat], axis=1)
    preact = far + jnp.dot(
        rest, w_in[width:], precision=highest, preferred_element_type=jnp.float32
    )
    sigma = jax.nn.sigmoid(preact)
    hidden = preact * sigma
    back = jnp.dot(upstream, w_out.T, precision=highest, preferred_element_type=jnp.float32)
    dpre = back * sigma * (1.0 + preact * (1.0 - sigma))
    grad_second = jnp.dot(hidden.T, upstream, precision=highest, preferred_element_type=jnp.float32)
    grad_rest = jnp.dot(rest.T, dpre, precision=highest, preferred_element_type=jnp.float32)
    drest = jnp.dot(dpre, w_in[width:].T, precision=highest, preferred_element_type=jnp.float32)
    hot = (
        source[:, None] == jnp.arange(lax.axis_size("edge") * node_rows, dtype=jnp.int32)[None, :]
    ).astype(jnp.float32)
    source_sum = lax.psum_scatter(
        jnp.einsum("ec,ew->cw", hot, dpre, precision=highest, preferred_element_type=jnp.float32),
        "edge",
        scatter_dimension=0,
        tiled=True,
    )
    grad_source = jnp.dot(
        source_sum, w_source.T, precision=highest, preferred_element_type=jnp.float32
    )
    grad_top = jnp.dot(nodes.T, source_sum, precision=highest, preferred_element_type=jnp.float32)
    grad_first = jnp.concatenate([grad_top, grad_rest], axis=0)
    near_grad = drest[:, :width]
    grads = grad_source + jnp.einsum(
        "en,ew->nw", local_hot, near_grad, precision=highest, preferred_element_type=jnp.float32
    )
    grad_first, grad_second = lax.psum((grad_first, grad_second), "edge")
    factor = 1.0 / math.sqrt(edge_rows * devices)
    return (grads, grad_first * factor, grad_second * factor)


MESH = pl.DeviceIdType.MESH
NODE, COT, TGT, HID, SRC, FA, FB = range(7)


def split(value):
    high = value.astype(jnp.bfloat16)
    low = (value - high.astype(jnp.float32)).astype(jnp.bfloat16)
    return high, low


def mm(a, b, dims=((1,), (0,))):
    return lax.dot_general(a, b, (dims, ((), ())), preferred_element_type=jnp.float32)


def mm3(a, b, dims=((1,), (0,))):
    (ah, al), (bh, bl) = a, b
    return mm(ah, bh, dims) + (mm(ah, bl, dims) + mm(al, bh, dims))


def kernel(n, nodes_hbm, cot_hbm, src_hbm, tgt_hbm, feat_hbm, win_hbm, wout_hbm, grads, gin, gout,
           ag, part, rc, rx, rz, eth, etl, hot_t, hot,
           tabh, tabl, bkh, bkl, pre, dh, dl, ngth, ngtl, src, tgt, nodes, cot, feat, win, wout, load_sem, send_sem, recv_sem):
    f32, bf16 = jnp.float32, jnp.bfloat16
    rows, width = nodes.shape
    edges = src.shape[1]
    zs = n // 4
    total = n * rows
    factor = 1.0 / math.sqrt(edges * n)
    me = lax.axis_index("edge")
    c, x, z = lax.rem(me, 2), lax.rem(me // 2, 2), me // 4

    def index(z, x, c):
        return (z * 2 + x) * 2 + c

    sibling, across = index(z, x, 1 - c), index(z, 1 - x, c)
    line = [index(lax.rem(z + k, zs), x, c) for k in range(1, zs)]
    half, quarter = total // 2, total // 4

    def at(size, start):
        return pl.ds(pl.multiple_of(start, rows), size)

    own = at(rows, c * half + x * quarter + z * rows)
    sent = {}

    def send(key, slot, source, dest, device):
        copy = pltpu.make_async_remote_copy(
            src_ref=source, dst_ref=dest, send_sem=send_sem.at[slot], recv_sem=recv_sem.at[slot],
            device_id={"edge": device}, device_id_type=MESH)
        copy.start()
        sent.setdefault(key, []).append(copy)

    def fin(*key):
        for copy in sent[key]:
            copy.wait_recv()

    per = zs + 1

    def cols(h):
        return pl.ds(0, width) if h is None else pl.ds(h * (width // 2), width // 2)

    def slot(i, h):
        return i * per if not h else (10 + i) * per

    def ag_z(i, h=None):
        for k, device in enumerate(line):
            send(("az", i, h), slot(i, h) + k, ag.at[i, own, cols(h)], ag.at[i, own, cols(h)],
                 device)

    def ag_x(i, h=None):
        fin("az", i, h)
        block = at(quarter, c * half + x * quarter)
        send(("ax", i, h), slot(i, h) + zs - 1, ag.at[i, block, cols(h)], ag.at[i, block, cols(h)],
             across)

    def ag_c(i, h=None):
        fin("ax", i, h)
        block = at(half, c * half)
        send(("ac", i, h), slot(i, h) + zs, ag.at[i, block, cols(h)], ag.at[i, block, cols(h)],
             sibling)

    def rs_c(j):
        send(("rc", j), (7 + j) * per, part.at[j, at(half, (1 - c) * half)], rc.at[j], sibling)

    def rs_x(j):
        fin("rc", j)
        away = at(quarter, c * half + (1 - x) * quarter)
        part[j, away] += rc[j, at(quarter, (1 - x) * quarter)]
        send(("rx", j), (7 + j) * per + 1, part.at[j, away], rx.at[j], across)
        part[j, at(quarter, c * half + x * quarter)] += rc[j, at(quarter, x * quarter)]

    def rs_z(j):
        fin("rx", j)
        base = c * half + x * quarter
        part[j, at(quarter, base)] += rx[j]
        for k, device in enumerate(line):
            other = lax.rem(z + k + 1, zs)
            send(("rz", j), (7 + j) * per + 2 + k, part.at[j, at(rows, base + other * rows)],
                 rz.at[j, k], device)

    def rs_done(j, i):
        fin("rz", j)
        piece = part[j, own]
        for k in range(zs - 1):
            piece = piece + rz[j, k]
        ag[i, own] = piece
        ag_z(i)

    load_small = [
        pltpu.make_async_copy(src_hbm, src.at[0], load_sem.at[0]),
        pltpu.make_async_copy(tgt_hbm, tgt.at[0], load_sem.at[1]),
    ]
    load_rows = [
        pltpu.make_async_copy(nodes_hbm, nodes, load_sem.at[2]),
        pltpu.make_async_copy(cot_hbm, cot, load_sem.at[3]),
    ]
    load_big = [
        pltpu.make_async_copy(feat_hbm, feat, load_sem.at[4]),
        pltpu.make_async_copy(win_hbm, win, load_sem.at[5]),
        pltpu.make_async_copy(wout_hbm, wout, load_sem.at[6]),
    ]
    for copy in load_rows + load_small + load_big:
        copy.start()
    barrier = pltpu.get_barrier_semaphore()
    peers = [sibling, across] + line
    for device in peers:
        pl.semaphore_signal(barrier, inc=1, device_id={"edge": device}, device_id_type=MESH)
    for copy in load_rows:
        copy.wait()
    ag[NODE, own] = nodes[...]
    ag[COT, own] = cot[...]
    pl.semaphore_wait(barrier, len(peers))
    for h in range(2):
        ag_z(NODE, h)
    for copy in load_small:
        copy.wait()

    ids = src[...]
    owner = ids // rows
    place = (lax.rem(owner, 2) * half + lax.rem(owner // 2, 2) * quarter
             + (owner // 4) * rows + lax.rem(ids, rows))
    seen = lax.broadcasted_iota(jnp.int32, (total, edges), 0) == place
    near = lax.broadcasted_iota(jnp.int32, (128, edges), 0) == tgt[...] - me * rows
    seen, near = jnp.where(seen, 1.0, 0.0), jnp.where(near, 1.0, 0.0)
    hot_t[0:total] = seen.astype(bf16)
    hot_t[total:total + 128] = near.astype(bf16)
    hot[:, 0:total] = seen.T.astype(bf16)
    hot[:, total:total + 128] = near.T.astype(bf16)

    tile = 256
    tiles = edges // tile

    def turn(t):
        high, low = split(feat[t * tile:(t + 1) * tile].T)
        eth[:, t * tile:(t + 1) * tile] = high
        etl[:, t * tile:(t + 1) * tile] = low

    for h in range(2):
        ag_x(NODE, h)
    ag_z(COT)
    for copy in load_big:
        copy.wait()
    pre[...] = mm3(split(feat[...]), split(win[2 * width:3 * width]))
    for h in range(2):
        ag_c(NODE, h)
    zeros = jnp.zeros((128 - rows, width), bf16)
    th, tl = split(mm3(split(nodes[...]), split(win[width:2 * width])))
    tabh[total:total + 128] = jnp.concatenate([th, zeros], axis=0)
    tabl[total:total + 128] = jnp.concatenate([tl, zeros], axis=0)
    th, tl = split(mm3(split(cot[...]), split(wout[...]), ((1,), (1,))))
    bkh[...] = jnp.concatenate([th, zeros], axis=0)
    bkl[...] = jnp.concatenate([tl, zeros], axis=0)
    for t in range(tiles):
        turn(t)
    for h in range(2):
        fin("ac", NODE, h)
    th, tl = split(mm3(split(ag[NODE]), split(win[0:width])))
    tabh[0:total] = th
    tabl[0:total] = tl
    ag_x(COT)

    t_sum = jnp.zeros((rows, width), f32)
    g_sum = jnp.zeros((rows, width), f32)
    for t in range(tiles):
        cut = slice(t * tile, (t + 1) * tile)
        ones = hot[cut]
        v = pre[cut] + (mm(ones, tabh[...]) + mm(ones, tabl[...]))
        back = mm(ones[:, total:], bkh[...]) + mm(ones[:, total:], bkl[...])
        sigma = jax.nn.sigmoid(v)
        hh, hl = split(v * sigma)
        high, low = split(back * sigma * (1.0 + v * (1.0 - sigma)))
        dh[cut] = high
        dl[cut] = low
        ones_t = hot_t[total:total + rows, cut]
        t_sum += mm(ones_t, high) + mm(ones_t, low)
        g_sum += mm(ones_t, hh) + mm(ones_t, hl)
    ag[TGT, own] = t_sum
    ag[HID, own] = g_sum
    ag_z(TGT)
    ag_z(HID)

    def partial(j, side):
        place = at(half, side * half)
        if j == 0:
            ones_t = hot_t[place]
            part[j, place] = mm(ones_t, dh[...]) + mm(ones_t, dl[...])
        else:
            cut = at(half, (j - 1) * total + side * half)
            part[j, place] = mm3((eth[cut], etl[cut]), (dh[...], dl[...]))

    for j in range(3):
        partial(j, 1 - c)
        rs_c(j)
    partial(0, c)
    rs_x(0)
    partial(1, c)
    rs_x(1)
    partial(2, c)
    ag_c(COT)
    rs_z(0)
    rs_x(2)
    ag_x(TGT)
    ag_x(HID)
    nh, nl = split(ag[NODE].T)
    ngth[...] = nh
    ngtl[...] = nl
    rs_z(1)
    rs_done(0, SRC)
    rs_z(2)
    ag_c(TGT)
    ag_c(HID)
    grads[...] = (mm3(split(ag[SRC, own]), split(win[0:width]), ((1,), (1,)))
                  + mm3(split(ag[TGT, own]), split(win[width:2 * width]), ((1,), (1,))))
    rs_done(1, FA)
    ag_x(SRC)
    rs_done(2, FB)
    fin("ac", TGT, None)
    gin[width:2 * width] = mm3((ngth[...], ngtl[...]), split(ag[TGT])) * factor
    ag_x(FA)
    ag_c(SRC)
    ag_x(FB)
    fin("ac", HID, None)
    fin("ac", COT, None)
    gout[...] = mm3(split(ag[HID].T), split(ag[COT])) * factor
    ag_c(FA)
    fin("ac", SRC, None)
    gin[0:width] = mm3((ngth[...], ngtl[...]), split(ag[SRC])) * factor
    ag_c(FB)
    fin("ac", FA, None)
    gin[2 * width:2 * width + total] = ag[FA] * factor
    fin("ac", FB, None)
    gin[2 * width + total:3 * width] = ag[FB] * factor
    for copies in sent.values():
        for copy in copies:
            copy.wait_send()


def write_out(*refs):
    sem = refs[6]
    copies = [pltpu.make_async_copy(refs[k], refs[3 + k], sem.at[k]) for k in range(3)]
    for copy in copies:
        copy.start()
    for copy in copies:
        copy.wait()


def fused(n, nodes, edge_feat, source, target, w_in, w_out, cotangent):
    f32, bf16 = jnp.float32, jnp.bfloat16
    rows, width = nodes.shape
    edges = source.shape[0]
    zs, total = n // 4, n * rows
    vmem = pl.BlockSpec(memory_space=pltpu.VMEM)
    hbm = pl.BlockSpec(memory_space=pl.ANY)
    scratch = [
        ((7, total, width), f32), ((3, total, width), f32), ((3, total // 2, width), f32),
        ((3, total // 4, width), f32), ((3, zs - 1, rows, width), f32),
        ((width, edges), bf16), ((width, edges), bf16),
        ((total + 128, edges), bf16), ((edges, total + 128), bf16),
        ((total + 128, width), bf16), ((total + 128, width), bf16),
        ((128, width), bf16), ((128, width), bf16),
        ((edges, width), f32), ((edges, width), bf16), ((edges, width), bf16),
        ((width, total), bf16), ((width, total), bf16),
        ((1, edges), jnp.int32), ((1, edges), jnp.int32),
        ((rows, width), f32), ((rows, width), f32),
        ((edges, width), f32), ((3 * width, width), f32), ((width, width), f32),
    ]
    copies = 11 * (zs + 1)
    results = pl.pallas_call(
        functools.partial(kernel, n),
        out_shape=(
            jax.ShapeDtypeStruct((rows, width), f32),
            jax.ShapeDtypeStruct((3 * width, width), f32),
            jax.ShapeDtypeStruct((width, width), f32),
        ),
        in_specs=[hbm] * 7,
        out_specs=(vmem, vmem, vmem),
        scratch_shapes=[pltpu.VMEM(shape, kind) for shape, kind in scratch] + [
            pltpu.SemaphoreType.DMA((7,)),
            pltpu.SemaphoreType.DMA((copies,)),
            pltpu.SemaphoreType.DMA((copies,)),
        ],
        compiler_params=pltpu.CompilerParams(
            collective_id=0, has_side_effects=True, vmem_limit_bytes=32 * 2**20),
    )(*[pltpu.with_memory_space_constraint(value, pltpu.HBM) for value in (
        nodes, cotangent, source, target, edge_feat, w_in, w_out)])
    return pl.pallas_call(
        write_out,
        out_shape=tuple(jax.ShapeDtypeStruct(r.shape, r.dtype) for r in results),
        in_specs=[hbm] * 3,
        out_specs=(hbm,) * 3,
        scratch_shapes=[pltpu.SemaphoreType.DMA((3,))],
        compiler_params=pltpu.CompilerParams(vmem_limit_bytes=2 * 2**20),
    )(*results)


def body(nodes, edge_feat, source, target, w_in, w_out, cotangent):
    devices = lax.axis_size("edge")
    rows, width = nodes.shape
    if devices % 4 == 0 and devices >= 8 and 2 * devices * rows == width and source.shape[0] % 256 == 0:
        return fused(devices, nodes, edge_feat, source, target, w_in, w_out, cotangent)
    return plain(nodes, edge_feat, source, target, w_in, w_out, cotangent)


def solution(mesh):
    placed = (
        P(("groups", "edge"), None),
        P(("groups", "edge"), None),
        P(("groups", "edge")),
        P(("groups", "edge")),
        P(),
        P(),
        P(("groups", "edge"), None),
    )
    return jax.shard_map(
        body,
        mesh=mesh,
        in_specs=placed,
        out_specs=(P(("groups", "edge"), None), P("groups", None), P("groups", None)),
        check_vma=False,
    )
```

```python
import functools
import math

import jax
import jax.numpy as jnp
from jax import lax
from jax.experimental import pallas as pl
from jax.experimental.pallas import tpu as pltpu
from jax.sharding import PartitionSpec as P


def plain(nodes, edge_feat, source, target, w_in, w_out, cotangent):
    highest = lax.Precision.HIGHEST
    node_rows, width = nodes.shape
    edge_rows = source.shape[0]
    devices = lax.axis_size("edge")
    first_node = lax.axis_index("edge") * node_rows
    local_hot = (
        target[:, None] - first_node == jnp.arange(node_rows, dtype=jnp.int32)[None, :]
    ).astype(jnp.float32)
    near = jnp.dot(local_hot, nodes, precision=highest, preferred_element_type=jnp.float32)
    upstream = jnp.dot(local_hot, cotangent, precision=highest, preferred_element_type=jnp.float32)
    w_source = w_in[:width]
    table = jnp.dot(nodes, w_source, precision=highest, preferred_element_type=jnp.float32)
    piece = lax.all_gather(table, "edge", axis=0, tiled=True)
    count = piece.shape[0]
    hot = (source[:, None] == jnp.arange(count, dtype=jnp.int32)[None, :]).astype(jnp.float32)
    far = jnp.dot(hot, piece, precision=highest, preferred_element_type=jnp.float32)
    rest = jnp.concatenate([near, edge_feat], axis=1)
    preact = far + jnp.dot(
        rest, w_in[width:], precision=highest, preferred_element_type=jnp.float32
    )
    sigma = jax.nn.sigmoid(preact)
    hidden = preact * sigma
    back = jnp.dot(upstream, w_out.T, precision=highest, preferred_element_type=jnp.float32)
    dpre = back * sigma * (1.0 + preact * (1.0 - sigma))
    grad_second = jnp.dot(hidden.T, upstream, precision=highest, preferred_element_type=jnp.float32)
    grad_rest = jnp.dot(rest.T, dpre, precision=highest, preferred_element_type=jnp.float32)
    drest = jnp.dot(dpre, w_in[width:].T, precision=highest, preferred_element_type=jnp.float32)
    hot = (
        source[:, None] == jnp.arange(lax.axis_size("edge") * node_rows, dtype=jnp.int32)[None, :]
    ).astype(jnp.float32)
    source_sum = lax.psum_scatter(
        jnp.einsum("ec,ew->cw", hot, dpre, precision=highest, preferred_element_type=jnp.float32),
        "edge",
        scatter_dimension=0,
        tiled=True,
    )
    grad_source = jnp.dot(
        source_sum, w_source.T, precision=highest, preferred_element_type=jnp.float32
    )
    grad_top = jnp.dot(nodes.T, source_sum, precision=highest, preferred_element_type=jnp.float32)
    grad_first = jnp.concatenate([grad_top, grad_rest], axis=0)
    near_grad = drest[:, :width]
    grads = grad_source + jnp.einsum(
        "en,ew->nw", local_hot, near_grad, precision=highest, preferred_element_type=jnp.float32
    )
    grad_first, grad_second = lax.psum((grad_first, grad_second), "edge")
    factor = 1.0 / math.sqrt(edge_rows * devices)
    return (grads, grad_first * factor, grad_second * factor)


MESH = pl.DeviceIdType.MESH
NODE, COT, TGT, HID, SRC, FA, FB = range(7)


def split(value):
    high = value.astype(jnp.bfloat16)
    low = (value - high.astype(jnp.float32)).astype(jnp.bfloat16)
    return high, low


def mm(a, b, dims=((1,), (0,))):
    return lax.dot_general(a, b, (dims, ((), ())), preferred_element_type=jnp.float32)


def mm3(a, b, dims=((1,), (0,))):
    (ah, al), (bh, bl) = a, b
    return mm(ah, bh, dims) + (mm(ah, bl, dims) + mm(al, bh, dims))


def kernel(n, nodes_hbm, cot_hbm, src_hbm, tgt_hbm, feat_hbm, win_hbm, wout_hbm, grads, gin, gout,
           ag, part, rc, rx, rz, eth, etl, hot_t, hot,
           tabh, tabl, bkh, bkl, pre, dh, dl, ngth, ngtl, src, tgt, nodes, cot, feat, win, wout, load_sem, send_sem, recv_sem):
    f32, bf16 = jnp.float32, jnp.bfloat16
    rows, width = nodes.shape
    edges = src.shape[1]
    zs = n // 4
    total = n * rows
    factor = 1.0 / math.sqrt(edges * n)
    me = lax.axis_index("edge")
    c, x, z = lax.rem(me, 2), lax.rem(me // 2, 2), me // 4

    def index(z, x, c):
        return (z * 2 + x) * 2 + c

    sibling, across = index(z, x, 1 - c), index(z, 1 - x, c)
    line = [index(lax.rem(z + k, zs), x, c) for k in range(1, zs)]
    half, quarter = total // 2, total // 4

    def at(size, start):
        return pl.ds(pl.multiple_of(start, rows), size)

    own = at(rows, c * half + x * quarter + z * rows)
    sent = {}

    def send(key, slot, source, dest, device):
        copy = pltpu.make_async_remote_copy(
            src_ref=source, dst_ref=dest, send_sem=send_sem.at[slot], recv_sem=recv_sem.at[slot],
            device_id={"edge": device}, device_id_type=MESH)
        copy.start()
        sent.setdefault(key, []).append(copy)

    def fin(*key):
        for copy in sent[key]:
            copy.wait_recv()

    per = zs + 1

    def cols(h):
        return pl.ds(0, width) if h is None else pl.ds(h * (width // 2), width // 2)

    def slot(i, h):
        return i * per if not h else (10 + i) * per

    def ag_z(i, h=None):
        for k, device in enumerate(line):
            send(("az", i, h), slot(i, h) + k, ag.at[i, own, cols(h)], ag.at[i, own, cols(h)],
                 device)

    def ag_x(i, h=None):
        fin("az", i, h)
        block = at(quarter, c * half + x * quarter)
        send(("ax", i, h), slot(i, h) + zs - 1, ag.at[i, block, cols(h)], ag.at[i, block, cols(h)],
             across)

    def ag_c(i, h=None):
        fin("ax", i, h)
        block = at(half, c * half)
        send(("ac", i, h), slot(i, h) + zs, ag.at[i, block, cols(h)], ag.at[i, block, cols(h)],
             sibling)

    def rs_c(j):
        send(("rc", j), (7 + j) * per, part.at[j, at(half, (1 - c) * half)], rc.at[j], sibling)

    def rs_x(j):
        fin("rc", j)
        away = at(quarter, c * half + (1 - x) * quarter)
        part[j, away] += rc[j, at(quarter, (1 - x) * quarter)]
        send(("rx", j), (7 + j) * per + 1, part.at[j, away], rx.at[j], across)
        part[j, at(quarter, c * half + x * quarter)] += rc[j, at(quarter, x * quarter)]

    def rs_z(j):
        fin("rx", j)
        base = c * half + x * quarter
        part[j, at(quarter, base)] += rx[j]
        for k, device in enumerate(line):
            other = lax.rem(z + k + 1, zs)
            send(("rz", j), (7 + j) * per + 2 + k, part.at[j, at(rows, base + other * rows)],
                 rz.at[j, k], device)

    def rs_done(j, i, parts=(None,)):
        fin("rz", j)
        piece = part[j, own]
        for k in range(zs - 1):
            piece = piece + rz[j, k]
        ag[i, own] = piece
        for h in parts:
            ag_z(i, h)

    load_small = [
        pltpu.make_async_copy(src_hbm, src.at[0], load_sem.at[0]),
        pltpu.make_async_copy(tgt_hbm, tgt.at[0], load_sem.at[1]),
    ]
    load_rows = [
        pltpu.make_async_copy(nodes_hbm, nodes, load_sem.at[2]),
        pltpu.make_async_copy(cot_hbm, cot, load_sem.at[3]),
    ]
    load_big = [
        pltpu.make_async_copy(feat_hbm, feat, load_sem.at[4]),
        pltpu.make_async_copy(win_hbm, win, load_sem.at[5]),
        pltpu.make_async_copy(wout_hbm, wout, load_sem.at[6]),
    ]
    for copy in load_rows + load_small + load_big:
        copy.start()
    barrier = pltpu.get_barrier_semaphore()
    peers = [sibling, across] + line
    for device in peers:
        pl.semaphore_signal(barrier, inc=1, device_id={"edge": device}, device_id_type=MESH)
    for copy in load_rows:
        copy.wait()
    ag[NODE, own] = nodes[...]
    ag[COT, own] = cot[...]
    pl.semaphore_wait(barrier, len(peers))
    for h in range(2):
        ag_z(NODE, h)
    for copy in load_small:
        copy.wait()

    ids = src[...]
    owner = ids // rows
    place = (lax.rem(owner, 2) * half + lax.rem(owner // 2, 2) * quarter
             + (owner // 4) * rows + lax.rem(ids, rows))
    seen = lax.broadcasted_iota(jnp.int32, (total, edges), 0) == place
    near = lax.broadcasted_iota(jnp.int32, (128, edges), 0) == tgt[...] - me * rows
    seen, near = jnp.where(seen, 1.0, 0.0), jnp.where(near, 1.0, 0.0)
    hot_t[0:total] = seen.astype(bf16)
    hot_t[total:total + 128] = near.astype(bf16)
    hot[:, 0:total] = seen.T.astype(bf16)
    hot[:, total:total + 128] = near.T.astype(bf16)

    tile = 256
    tiles = edges // tile

    def turn(t):
        high, low = split(feat[t * tile:(t + 1) * tile].T)
        eth[:, t * tile:(t + 1) * tile] = high
        etl[:, t * tile:(t + 1) * tile] = low

    for h in range(2):
        ag_x(NODE, h)
    ag_z(COT)
    for copy in load_big:
        copy.wait()
    pre[...] = mm3(split(feat[...]), split(win[2 * width:3 * width]))
    for h in range(2):
        ag_c(NODE, h)
    zeros = jnp.zeros((128 - rows, width), bf16)
    th, tl = split(mm3(split(nodes[...]), split(win[width:2 * width])))
    tabh[total:total + 128] = jnp.concatenate([th, zeros], axis=0)
    tabl[total:total + 128] = jnp.concatenate([tl, zeros], axis=0)
    th, tl = split(mm3(split(cot[...]), split(wout[...]), ((1,), (1,))))
    bkh[...] = jnp.concatenate([th, zeros], axis=0)
    bkl[...] = jnp.concatenate([tl, zeros], axis=0)
    for t in range(tiles):
        turn(t)
    for h in range(2):
        fin("ac", NODE, h)
    th, tl = split(mm3(split(ag[NODE]), split(win[0:width])))
    tabh[0:total] = th
    tabl[0:total] = tl
    ag_x(COT)

    t_sum = jnp.zeros((rows, width), f32)
    g_sum = jnp.zeros((rows, width), f32)
    for t in range(tiles):
        cut = slice(t * tile, (t + 1) * tile)
        ones = hot[cut]
        v = pre[cut] + (mm(ones, tabh[...]) + mm(ones, tabl[...]))
        back = mm(ones[:, total:], bkh[...]) + mm(ones[:, total:], bkl[...])
        sigma = jax.nn.sigmoid(v)
        hh, hl = split(v * sigma)
        high, low = split(back * sigma * (1.0 + v * (1.0 - sigma)))
        dh[cut] = high
        dl[cut] = low
        ones_t = hot_t[total:total + rows, cut]
        t_sum += mm(ones_t, high) + mm(ones_t, low)
        g_sum += mm(ones_t, hh) + mm(ones_t, hl)
    ag[TGT, own] = t_sum
    ag[HID, own] = g_sum
    ag_z(TGT)
    ag_z(HID)

    def partial(j, side):
        place = at(half, side * half)
        if j == 0:
            ones_t = hot_t[place]
            part[j, place] = mm(ones_t, dh[...]) + mm(ones_t, dl[...])
        else:
            cut = at(half, (j - 1) * total + side * half)
            part[j, place] = mm3((eth[cut], etl[cut]), (dh[...], dl[...]))

    for j in range(3):
        partial(j, 1 - c)
        rs_c(j)
    partial(0, c)
    rs_x(0)
    partial(1, c)
    rs_x(1)
    partial(2, c)
    ag_c(COT)
    rs_z(0)
    rs_x(2)
    ag_x(TGT)
    ag_x(HID)
    nh, nl = split(ag[NODE].T)
    ngth[...] = nh
    ngtl[...] = nl
    rs_z(1)
    rs_done(0, SRC)
    rs_z(2)
    rs_done(1, FA)
    ag_x(SRC)
    ag_c(TGT)
    rs_done(2, FB, (0, 1))
    ag_c(HID)
    ag_x(FA)
    fin("ac", TGT, None)
    gin[width:2 * width] = mm3((ngth[...], ngtl[...]), split(ag[TGT])) * factor
    ag_x(FB, 0)
    ag_x(FB, 1)
    ag_c(SRC)
    grads[...] = (mm3(split(ag[SRC, own]), split(win[0:width]), ((1,), (1,)))
                  + mm3(split(ag[TGT, own]), split(win[width:2 * width]), ((1,), (1,))))
    fin("ac", HID, None)
    fin("ac", COT, None)
    gout[...] = mm3(split(ag[HID].T), split(ag[COT])) * factor
    ag_c(FA)
    fin("ac", SRC, None)
    gin[0:width] = mm3((ngth[...], ngtl[...]), split(ag[SRC])) * factor
    ag_c(FB, 0)
    fin("ac", FA, None)
    gin[2 * width:2 * width + total] = ag[FA] * factor
    ag_c(FB, 1)
    for h in range(2):
        fin("ac", FB, h)
        gin[2 * width + total:3 * width, cols(h)] = ag[FB, :, cols(h)] * factor
    for copies in sent.values():
        for copy in copies:
            copy.wait_send()


def write_out(*refs):
    sem = refs[6]
    copies = [pltpu.make_async_copy(refs[k], refs[3 + k], sem.at[k]) for k in range(3)]
    for copy in copies:
        copy.start()
    for copy in copies:
        copy.wait()


def fused(n, nodes, edge_feat, source, target, w_in, w_out, cotangent):
    f32, bf16 = jnp.float32, jnp.bfloat16
    rows, width = nodes.shape
    edges = source.shape[0]
    zs, total = n // 4, n * rows
    vmem = pl.BlockSpec(memory_space=pltpu.VMEM)
    hbm = pl.BlockSpec(memory_space=pl.ANY)
    scratch = [
        ((7, total, width), f32), ((3, total, width), f32), ((3, total // 2, width), f32),
        ((3, total // 4, width), f32), ((3, zs - 1, rows, width), f32),
        ((width, edges), bf16), ((width, edges), bf16),
        ((total + 128, edges), bf16), ((edges, total + 128), bf16),
        ((total + 128, width), bf16), ((total + 128, width), bf16),
        ((128, width), bf16), ((128, width), bf16),
        ((edges, width), f32), ((edges, width), bf16), ((edges, width), bf16),
        ((width, total), bf16), ((width, total), bf16),
        ((1, edges), jnp.int32), ((1, edges), jnp.int32),
        ((rows, width), f32), ((rows, width), f32),
        ((edges, width), f32), ((3 * width, width), f32), ((width, width), f32),
    ]
    copies = 17 * (zs + 1)
    results = pl.pallas_call(
        functools.partial(kernel, n),
        out_shape=(
            jax.ShapeDtypeStruct((rows, width), f32),
            jax.ShapeDtypeStruct((3 * width, width), f32),
            jax.ShapeDtypeStruct((width, width), f32),
        ),
        in_specs=[hbm] * 7,
        out_specs=(vmem, vmem, vmem),
        scratch_shapes=[pltpu.VMEM(shape, kind) for shape, kind in scratch] + [
            pltpu.SemaphoreType.DMA((7,)),
            pltpu.SemaphoreType.DMA((copies,)),
            pltpu.SemaphoreType.DMA((copies,)),
        ],
        compiler_params=pltpu.CompilerParams(
            collective_id=0, has_side_effects=True, vmem_limit_bytes=32 * 2**20),
    )(*[pltpu.with_memory_space_constraint(value, pltpu.HBM) for value in (
        nodes, cotangent, source, target, edge_feat, w_in, w_out)])
    return pl.pallas_call(
        write_out,
        out_shape=tuple(jax.ShapeDtypeStruct(r.shape, r.dtype) for r in results),
        in_specs=[hbm] * 3,
        out_specs=(hbm,) * 3,
        scratch_shapes=[pltpu.SemaphoreType.DMA((3,))],
        compiler_params=pltpu.CompilerParams(vmem_limit_bytes=2 * 2**20),
    )(*results)


def body(nodes, edge_feat, source, target, w_in, w_out, cotangent):
    devices = lax.axis_size("edge")
    rows, width = nodes.shape
    if devices % 4 == 0 and devices >= 8 and 2 * devices * rows == width and source.shape[0] % 256 == 0:
        return fused(devices, nodes, edge_feat, source, target, w_in, w_out, cotangent)
    return plain(nodes, edge_feat, source, target, w_in, w_out, cotangent)


def solution(mesh):
    placed = (
        P(("groups", "edge"), None),
        P(("groups", "edge"), None),
        P(("groups", "edge")),
        P(("groups", "edge")),
        P(),
        P(),
        P(("groups", "edge"), None),
    )
    return jax.shard_map(
        body,
        mesh=mesh,
        in_specs=placed,
        out_specs=(P(("groups", "edge"), None), P("groups", None), P("groups", None)),
        check_vma=False,
    )
```
